32 devices in a mesh: row: 8 (over y, x, core), col: 4 (over z).
Axes of the slice: x: 2, y: 2, z: 4, core: 2. Of those that a mesh axis runs over, the one named last changes fastest.
Arguments:
- features: float32 [8192, 256], P(('row', 'col')), may hold values from -6 to 6
- loader_perm: int32 [8192], P(('row', 'col')), may hold values from 0 to 8191, as said below
- block_values: float32 [8, 4, 256, 4096], P('row', 'col'), may hold values from -0.09375 to 0.09375
- block_row: int32 [8, 4, 256], P('row', 'col'), may hold values from 0 to 31
- block_column: int32 [8, 4, 256], P('row', 'col'), may hold values from 0 to 15
- tile_count: int32 [8, 4], P('row', 'col'), may hold values from 32 to 256, as said below
- weight: float32 [256, 256], replicated, may hold values from -0.375 to 0.375
- bias_vector: float32 [256], replicated, may hold values from -0.5 to 0.5
- cotangent: float32 [8192, 256], P(('row', 'col')), may hold values from -6 to 6
Outputs:
- output: float32 [8192, 256], P(('row', 'col'))
- grad_x: float32 [8192, 256], P(('row', 'col'))
- grad_w: float32 [256, 256], replicated
- grad_b: float32 [256], replicated
The draws below stay inside these ranges and needn't reach their ends.
Inputs may be any that keep to these rules, and one draw needn't show every extreme that they name: `loader_perm`: every grid position appears once; the 256 loader rows of any one device name the same number of positions, 256 divided by the number of devices, in each aligned block of 256 grid positions. `tile_count`: every count is 256 divided by 1, 2, 4 or 8; a block position may appear in several slots of a tile, and such blocks add.
All inputs are finite; a program needn't handle non-finite values.
Results may differ from the reference program's by a relative error of at most 0.0003.
Values sent between devices are 32-bit elements; how exact they have to be, the bound alone decides.
A program may use at most 128 MiB of HBM per device.

```python
import math
import jax
import jax.numpy as jnp
from jax import lax

F = 256
BS = 64
NODE_DEV = 256
BLK_TILE = 256
NODES = 8192
N_ROW = 8
N_COL = 4


def draw_loader_perm(key, part):
    devices = N_ROW * N_COL
    per_device = NODE_DEV // devices
    key_dest = jax.random.fold_in(key, 11)
    key_source = jax.random.fold_in(key, 12)
    dest_perm = jax.vmap(lambda one_key: jax.random.permutation(one_key, NODE_DEV))(jax.random.split(key_dest, devices)).astype(jnp.int32)
    dest_index = jnp.arange(devices, dtype=jnp.int32)[None, :, None]
    source_index = jnp.arange(devices, dtype=jnp.int32)[:, None, None]
    within = jnp.arange(per_device, dtype=jnp.int32)[None, None, :]
    positions = dest_index * NODE_DEV + dest_perm[dest_index, source_index * per_device + within]
    positions = positions.reshape(devices, NODE_DEV)
    shuffle = jax.vmap(lambda one_key: jax.random.permutation(one_key, NODE_DEV))(jax.random.split(key_source, devices)).astype(jnp.int32)
    positions = jnp.take_along_axis(positions, shuffle, axis=1)
    return positions.reshape(-1).astype(jnp.int32)


def draw_tile_count(key, part):
    tiles = N_ROW * N_COL
    shifts = jax.random.randint(jax.random.fold_in(key, 21), (tiles,), 0, 4).astype(jnp.int32)
    first_tile = jax.random.randint(jax.random.fold_in(key, 22), (), 0, tiles).astype(jnp.int32)
    second_tile = (first_tile + 1 + jax.random.randint(jax.random.fold_in(key, 23), (), 0, tiles - 1).astype(jnp.int32)) % tiles
    shifts = shifts.at[first_tile].set(0).at[second_tile].set(3)
    counts = jnp.right_shift(jnp.full((tiles,), BLK_TILE, jnp.int32), shifts)
    return counts.reshape(N_ROW, N_COL).astype(jnp.int32)


def place_ends(entries, stream_key, smallest, high):
    longest = entries.shape.index(max(entries.shape))
    spots = []
    for shift in (0, 1):
        where = [jax.random.randint(jax.random.fold_in(stream_key, axis), (), 0, length) for axis, length in enumerate(entries.shape)]
        where[longest] = (where[longest] + shift) % entries.shape[longest]
        spots.append(tuple(where))
    return entries.at[spots[0]].set(smallest).at[spots[1]].set(high)


def steps_of(own_key, shape, shards, least, high):
    loudness = 1.0
    for axis_at, shards_of in shards:
        draws = jax.random.uniform(jax.random.fold_in(jax.random.fold_in(own_key, 6), axis_at), (shards_of,), jnp.float32, least / len(shards), high / len(shards))
        loudness = loudness * jnp.repeat(jnp.exp(draws), shape[axis_at] // shards_of).reshape((-1,) + (1,) * (len(shape) - 1 - axis_at))
    return loudness


def centred(own_key, shape, spread, most, pieces=(), held_as=jnp.bfloat16):
    array = jax.random.normal(own_key, shape, jnp.float32) * spread
    if len(pieces) > 0:
        array = steps_of(own_key, shape, pieces, -0.22, 0.18) * array
    return jnp.clip(array, min=-most, max=most).astype(held_as)


def setup_inputs(seed: int = 0) -> dict:
    splits = jax.random.split(jax.random.key(seed), 10)
    features = centred(splits[0], (NODES, F), 1.0, 6.0, ((0, 32),), jnp.float32)
    loader_perm = draw_loader_perm(jax.random.fold_in(splits[9], 71), 0)
    block_values = centred(splits[2], (N_ROW, N_COL, BLK_TILE, BS * BS), (BLK_TILE * BS * BS // NODE_DEV) ** -0.5, 0.09375, ((0, 8), (1, 4)), jnp.float32)
    block_row = place_ends(jax.random.randint(splits[3], (N_ROW, N_COL, BLK_TILE), 0, N_ROW * NODE_DEV // BS), jax.random.fold_in(splits[3], 1), 0, (N_ROW * NODE_DEV // BS) - 1).astype(jnp.int32)
    block_column = place_ends(jax.random.randint(splits[4], (N_ROW, N_COL, BLK_TILE), 0, N_COL * NODE_DEV // BS), jax.random.fold_in(splits[4], 1), 0, (N_COL * NODE_DEV // BS) - 1).astype(jnp.int32)
    tile_count = draw_tile_count(jax.random.fold_in(splits[9], 71), 0)
    weight = centred(splits[6], (F, F), F ** -0.5, 0.375, (), jnp.float32)
    bias_vector = jnp.clip(jax.random.uniform(splits[7], (F,), jnp.float32, -0.5, 0.5), -0.5, 0.5)
    cotangent = centred(splits[8], (NODES, F), 1.0, 6.0, ((0, 32),), jnp.float32)
    return dict(features=features, loader_perm=loader_perm, block_values=block_values, block_row=block_row, block_column=block_column, tile_count=tile_count, weight=weight, bias_vector=bias_vector, cotangent=cotangent)


precise = lax.Precision.HIGHEST

def aggregate(source, block_values, block_row, block_column, tile_count, transpose):
    offsets = jnp.arange(BS, dtype=jnp.int32)
    slots = jnp.arange(BLK_TILE, dtype=jnp.int32)

    def one_tile(accumulated, tile):
        tile_row = tile // N_COL
        tile_col = tile % N_COL
        tile_vals = block_values[tile_row, tile_col].astype(source.dtype).reshape(BLK_TILE, BS, BS)
        alive = (slots < tile_count[tile_row, tile_col]).astype(source.dtype)
        tile_vals = tile_vals * alive[:, None, None]
        row_first = block_row[tile_row, tile_col].astype(jnp.int32) * BS
        out_first = (row_first // NODE_DEV * N_COL + tile_col) * NODE_DEV + row_first % NODE_DEV
        in_first = tile_row * (N_COL * NODE_DEV) + block_column[tile_row, tile_col].astype(jnp.int32) * BS
        out_at = out_first[:, None] + offsets[None, :]
        in_at = in_first[:, None] + offsets[None, :]
        if transpose:
            terms = jnp.einsum('kba,kbf->kaf', tile_vals, source[out_at], precision=precise)
            return (accumulated.at[in_at].add(terms), None)
        terms = jnp.einsum('kab,kbf->kaf', tile_vals, source[in_at], precision=precise)
        return (accumulated.at[out_at].add(terms), None)
    tiles = jnp.arange(N_ROW * N_COL, dtype=jnp.int32)
    accumulated, _ = lax.scan(one_tile, jnp.zeros(source.shape, source.dtype), tiles)
    return accumulated

def reference(features, loader_perm, block_values, block_row, block_column, tile_count, weight, bias_vector, cotangent):
    grid = jnp.zeros(features.shape, features.dtype).at[loader_perm].set(features)
    hidden = aggregate(grid, block_values, block_row, block_column, tile_count, False)
    preact = jnp.dot(hidden, weight, precision=precise) + bias_vector
    squashed = jax.nn.sigmoid(preact)
    output = preact * squashed
    grad_pre = cotangent * squashed * (1.0 + preact * (1.0 - squashed))
    grad_hidden = jnp.dot(grad_pre, weight.T, precision=precise)
    grad_x = aggregate(grad_hidden, block_values, block_row, block_column, tile_count, True)
    norm_scale = 1.0 / math.sqrt(NODES)
    grad_w = jnp.einsum('nf,ng->fg', hidden, grad_pre, precision=precise) * norm_scale
    grad_b = lax.optimization_barrier(jnp.sum(grad_pre, axis=0)) * norm_scale
    return (output, grad_x, grad_w, grad_b)
```

```python
import math

import jax
import jax.numpy as jnp
from jax import lax
from jax.sharding import PartitionSpec as P

precise = lax.Precision.HIGHEST
three = lax.Precision.HIGH


def general(
    features,
    loader_perm,
    block_values,
    block_row,
    block_column,
    tile_count,
    weight,
    bias_vector,
    cotangent,
):
    node_dev, feat_width = features.shape
    row_devices = lax.axis_size("row")
    col_devices = lax.axis_size("col")
    devices = row_devices * col_devices
    row_index = lax.axis_index("row")
    group_rows = col_devices * node_dev
    tile_vals = block_values[0, 0]
    slots, entries = tile_vals.shape
    side = math.isqrt(entries)
    out_blocks = row_devices * node_dev // side
    in_blocks = group_rows // side
    per_group = node_dev // row_devices
    ordering = jnp.argsort(loader_perm // group_rows, stable=True)
    sent_rows = jnp.broadcast_to(
        features[ordering].reshape(row_devices, 1, per_group, feat_width),
        (row_devices, col_devices, per_group, feat_width),
    ).reshape(devices, per_group, feat_width)
    sent_ids = jnp.broadcast_to(
        loader_perm[ordering].astype(jnp.float32).reshape(row_devices, 1, per_group),
        (row_devices, col_devices, per_group),
    ).reshape(devices, per_group)
    got_rows, got_ids = (
        lax.all_to_all(sent_rows, ("row", "col"), split_axis=0, concat_axis=0, tiled=True),
        lax.all_to_all(sent_ids, ("row", "col"), split_axis=0, concat_axis=0, tiled=True),
    )
    spot = block_row[0, 0] * in_blocks + block_column[0, 0]
    alive = jnp.arange(slots, dtype=jnp.int32) < tile_count[0, 0]
    places = jnp.arange(out_blocks * in_blocks, dtype=jnp.int32)
    chosen = ((places[:, None] == spot[None, :]) & alive[None, :]).astype(jnp.float32)
    dense = jnp.dot(chosen, tile_vals, precision=three)
    dense = dense.reshape(out_blocks, in_blocks, side, side).transpose(0, 2, 1, 3)
    dense = dense.reshape(out_blocks * side, in_blocks * side)

    local_pos = got_ids.reshape(group_rows).astype(jnp.int32) - row_index * group_rows
    at = jnp.arange(group_rows, dtype=jnp.int32)
    panel = jnp.dot(
        (at[:, None] == local_pos[None, :]).astype(jnp.float32),
        got_rows.reshape(group_rows, feat_width),
        precision=precise,
    )
    partial_value = jnp.dot(dense, panel, precision=three)
    hidden = lax.psum_scatter(partial_value, "row", scatter_dimension=0, tiled=True)
    preact = jnp.dot(hidden, weight, precision=precise) + bias_vector
    squashed = jax.nn.sigmoid(preact)
    output = preact * squashed
    grad_pre = cotangent * squashed * (1.0 + preact * (1.0 - squashed))
    grad_hidden = jnp.dot(grad_pre, weight.T, precision=precise)
    column = lax.all_gather(grad_hidden, "row", axis=0, tiled=True)
    local_w = jnp.einsum("nf,ng->fg", hidden, grad_pre, precision=precise)
    local_b = jnp.sum(grad_pre, axis=0)
    grad_w, grad_b = lax.psum((local_w, local_b), ("row", "col"))
    partial_x = jnp.einsum("nm,nf->mf", dense, column, precision=three)
    grad_x = lax.psum_scatter(partial_x, "col", scatter_dimension=0, tiled=True)
    norm_scale = 1.0 / math.sqrt(node_dev * devices)
    return (output, grad_x, grad_w * norm_scale, grad_b * norm_scale)


def solution(mesh):
    in_specs = (
        P(("row", "col"), None),
        P(("row", "col")),
        P("row", "col", None, None),
        P("row", "col", None),
        P("row", "col", None),
        P("row", "col"),
        P(),
        P(),
        P(("row", "col"), None),
    )
    out_specs = (P(("row", "col"), None), P(("row", "col"), None), P(), P())
    return jax.shard_map(
        general, mesh=mesh, in_specs=in_specs, out_specs=out_specs, check_vma=False
    )
```

```python
import functools
import math

import jax
import jax.numpy as jnp
from jax import lax
from jax.experimental import pallas as pl
from jax.experimental.pallas import tpu as pltpu
from jax.sharding import PartitionSpec as P

precise = lax.Precision.HIGHEST
three = lax.Precision.HIGH


def general(
    features,
    loader_perm,
    block_values,
    block_row,
    block_column,
    tile_count,
    weight,
    bias_vector,
    cotangent,
):
    node_dev, feat_width = features.shape
    row_devices = lax.axis_size("row")
    col_devices = lax.axis_size("col")
    devices = row_devices * col_devices
    row_index = lax.axis_index("row")
    group_rows = col_devices * node_dev
    tile_vals = block_values[0, 0]
    slots, entries = tile_vals.shape
    side = math.isqrt(entries)
    out_blocks = row_devices * node_dev // side
    in_blocks = group_rows // side
    per_group = node_dev // row_devices
    ordering = jnp.argsort(loader_perm // group_rows, stable=True)
    sent_rows = jnp.broadcast_to(
        features[ordering].reshape(row_devices, 1, per_group, feat_width),
        (row_devices, col_devices, per_group, feat_width),
    ).reshape(devices, per_group, feat_width)
    sent_ids = jnp.broadcast_to(
        loader_perm[ordering].astype(jnp.float32).reshape(row_devices, 1, per_group),
        (row_devices, col_devices, per_group),
    ).reshape(devices, per_group)
    got_rows, got_ids = (
        lax.all_to_all(sent_rows, ("row", "col"), split_axis=0, concat_axis=0, tiled=True),
        lax.all_to_all(sent_ids, ("row", "col"), split_axis=0, concat_axis=0, tiled=True),
    )
    spot = block_row[0, 0] * in_blocks + block_column[0, 0]
    alive = jnp.arange(slots, dtype=jnp.int32) < tile_count[0, 0]
    places = jnp.arange(out_blocks * in_blocks, dtype=jnp.int32)
    chosen = ((places[:, None] == spot[None, :]) & alive[None, :]).astype(jnp.float32)
    dense = jnp.dot(chosen, tile_vals, precision=three)
    dense = dense.reshape(out_blocks, in_blocks, side, side).transpose(0, 2, 1, 3)
    dense = dense.reshape(out_blocks * side, in_blocks * side)

    local_pos = got_ids.reshape(group_rows).astype(jnp.int32) - row_index * group_rows
    at = jnp.arange(group_rows, dtype=jnp.int32)
    panel = jnp.dot(
        (at[:, None] == local_pos[None, :]).astype(jnp.float32),
        got_rows.reshape(group_rows, feat_width),
        precision=precise,
    )
    partial_value = jnp.dot(dense, panel, precision=three)
    hidden = lax.psum_scatter(partial_value, "row", scatter_dimension=0, tiled=True)
    preact = jnp.dot(hidden, weight, precision=precise) + bias_vector
    squashed = jax.nn.sigmoid(preact)
    output = preact * squashed
    grad_pre = cotangent * squashed * (1.0 + preact * (1.0 - squashed))
    grad_hidden = jnp.dot(grad_pre, weight.T, precision=precise)
    column = lax.all_gather(grad_hidden, "row", axis=0, tiled=True)
    local_w = jnp.einsum("nf,ng->fg", hidden, grad_pre, precision=precise)
    local_b = jnp.sum(grad_pre, axis=0)
    grad_w, grad_b = lax.psum((local_w, local_b), ("row", "col"))
    partial_x = jnp.einsum("nm,nf->mf", dense, column, precision=three)
    grad_x = lax.psum_scatter(partial_x, "col", scatter_dimension=0, tiled=True)
    norm_scale = 1.0 / math.sqrt(node_dev * devices)
    return (output, grad_x, grad_w * norm_scale, grad_b * norm_scale)


def fused(
    node_dev, row_devices, col_devices, side,
    ids_row, ids_col, blk_row, blk_col, live, feats, vals_hbm, weight, bias, cotan,
    out, grad_x, grad_w, grad_b,
    sorted_rows, sorted_ids, got, got_ids, vals, tall, tile_hi, tile_lo, panel_hi, panel_lo,
    sent_part, core_part, summed, from_x, from_y, turned, late,
    column, column_hi, column_lo, sent_x, came_x, w_sent, w_came, w_line, w_full,
    vals_sem, fs, fr, fis, fir, zs, zr, zis, zir, cs, cr, xs, xr, ys, yr, ls, lr,
    ags, agr, ds, dr, ks, kr, gs, gr, ws, wr, wls, wlr, wfs, wfr,
):
    width = weight.shape[0]
    row, col = lax.axis_index("row"), lax.axis_index("col")
    core, chip = row % 2, row // 2
    x, y = chip % 2, chip // 2
    at_core = row + 1 - 2 * core
    at_x = row + 2 - 4 * x
    at_y = row + 4 - 8 * y
    at_diag = at_x + 4 - 8 * y
    half = node_dev // 2
    group_rows = col_devices * node_dev
    per = node_dev // row_devices
    slots = vals.shape[0]
    f32, bf16 = jnp.float32, jnp.bfloat16

    def remote(src, dst, ssem, rsem, **where):
        return pltpu.make_async_remote_copy(
            src_ref=src, dst_ref=dst, send_sem=ssem, recv_sem=rsem,
            device_id=where, device_id_type=pl.DeviceIdType.MESH,
        )

    def dot(a, b):
        return jnp.dot(a, b, preferred_element_type=f32)

    def exact(a, b):
        return jnp.dot(a, b, precision=precise, preferred_element_type=f32)

    def split(a):
        hi = a.astype(bf16)
        return hi, (a - hi.astype(f32)).astype(bf16)

    fetch = pltpu.make_async_copy(vals_hbm, vals, vals_sem)
    fetch.start()

    barrier = pltpu.get_barrier_semaphore()
    for t in range(1, row_devices):
        pl.semaphore_signal(
            barrier, inc=1, device_id={"row": (row + t) % row_devices},
            device_id_type=pl.DeviceIdType.MESH,
        )
    for t in range(1, col_devices):
        pl.semaphore_signal(
            barrier, inc=1, device_id={"col": (col + t) % col_devices},
            device_id_type=pl.DeviceIdType.MESH,
        )

    idr, idc = ids_row[...], ids_col[...]
    scale = 1.0 / group_rows
    grp_r, grp_c = jnp.floor(idr * scale), jnp.floor(idc * scale)
    sub = lax.broadcasted_iota(jnp.int32, (node_dev, node_dev), 0)
    lane = lax.broadcasted_iota(jnp.int32, (node_dev, node_dev), 1)
    same = grp_c == grp_r
    rank_r = jnp.sum(jnp.where(same & (sub < lane), 1.0, 0.0), axis=0, keepdims=True)
    rank_c = jnp.sum(jnp.where(same & (lane < sub), 1.0, 0.0), axis=1, keepdims=True)
    slot_r = grp_r * per + rank_r
    order = jnp.where(sub.astype(f32) == slot_r, 1.0, 0.0)
    moved = exact(order, feats[...])
    packed = 128 // per
    lane128 = lax.broadcasted_iota(jnp.int32, (node_dev, 128), 1)
    shift = ((row % packed) * per).astype(f32)
    placed = jnp.where(lane128.astype(f32) == rank_c + shift, 1.0, 0.0)
    dest = lax.broadcasted_iota(jnp.int32, (row_devices, node_dev), 0).astype(f32)
    id_rows = exact(jnp.where(dest == grp_r, idr, 0.0), placed)
    for d in range(row_devices):
        sorted_rows[d] = moved[d * per:(d + 1) * per]
        sorted_ids[d] = id_rows[d:d + 1]
    got[col, row] = sorted_rows[row]
    got_ids[col, row] = sorted_ids[row]

    pl.semaphore_wait(barrier, row_devices - 1 + col_devices - 1)
    first = []
    for t in range(1, row_devices):
        to = (row + t) % row_devices
        a = remote(sorted_rows.at[to], got.at[col, row], fs.at[t], fr.at[t], row=to)
        b = remote(sorted_ids.at[to], got_ids.at[col, row], fis.at[t], fir.at[t], row=to)
        a.start()
        b.start()
        first += [a, b]

    fetch.wait()

    count = live[...]
    slot_at = lax.broadcasted_iota(jnp.int32, (1, slots), 1)
    out_blocks = row_devices * node_dev // side
    in_blocks = group_rows // side
    key = jnp.where(slot_at < count, blk_col[...] * out_blocks + blk_row[...], -1)
    spot = lax.broadcasted_iota(jnp.int32, (out_blocks * in_blocks, slots), 0)
    chosen = jnp.where(spot == key, 1.0, 0.0).astype(bf16)
    left = lax.broadcasted_iota(jnp.int32, (out_blocks, 128), 1) < side

    def densify(step, carry):
        part = vals[:, pl.ds(pl.multiple_of(step * 256, 256), 256)]
        hi, lo = split(part)
        dense = dot(chosen, hi) + dot(chosen, lo)
        for pair in range(in_blocks // 2):
            top = dense[(2 * pair) * out_blocks:(2 * pair + 1) * out_blocks]
            low = dense[(2 * pair + 1) * out_blocks:(2 * pair + 2) * out_blocks]
            for h in range(2):
                p0, p1 = top[:, h * 128:(h + 1) * 128], low[:, h * 128:(h + 1) * 128]
                even = jnp.where(left, p0, pltpu.roll(p1, side, 1))
                odd = jnp.where(left, pltpu.roll(p0, side, 1), p1)
                at = step * 4 + h * 2
                tall[pair, pl.ds(at, out_blocks, stride=side), :] = even
                tall[pair, pl.ds(at + 1, out_blocks, stride=side), :] = odd
        return carry

    steps = vals.shape[1] // 256
    lax.fori_loop(0, steps // 2, densify, 0)

    for t in range(1, row_devices):
        frm = (row + row_devices - t) % row_devices
        remote(sorted_rows.at[frm], got.at[col, frm], fs.at[t], fr.at[t], row=frm).wait_recv()
        remote(sorted_ids.at[frm], got_ids.at[col, frm], fis.at[t], fir.at[t], row=frm).wait_recv()
    second = []
    for t in range(1, col_devices):
        to = (col + t) % col_devices
        a = remote(got.at[col], got.at[col], zs.at[t], zr.at[t], col=to)
        b = remote(got_ids.at[col], got_ids.at[col], zis.at[t], zir.at[t], col=to)
        a.start()
        b.start()
        second += [a, b]

    lax.fori_loop(steps // 2, steps, densify, 0)

    def narrow(i, carry):
        at = pl.multiple_of(i * node_dev, node_dev)
        for pair in range(in_blocks // 2):
            hi, lo = split(tall[pair, pl.ds(at, node_dev), :])
            tile_hi[pl.ds(at, node_dev), pair * 128:(pair + 1) * 128] = hi
            tile_lo[pl.ds(at, node_dev), pair * 128:(pair + 1) * 128] = lo
        return carry

    lax.fori_loop(0, row_devices, narrow, 0)

    for t in range(1, col_devices):
        frm = (col + col_devices - t) % col_devices
        remote(got.at[col], got.at[frm], zs.at[t], zr.at[t], col=frm).wait_recv()
        remote(got_ids.at[col], got_ids.at[frm], zis.at[t], zir.at[t], col=frm).wait_recv()

    pieces = []
    for j in range(col_devices):
        for s in range(0, row_devices, packed):
            pieces.append(sum(got_ids[j, s + k] for k in range(packed)))
    where = jnp.concatenate(pieces, axis=1) - (row * group_rows).astype(f32)
    got_hi, got_lo = split(got[...].reshape(group_rows, width))

    def place(i, carry):
        at = pl.multiple_of(i * node_dev, node_dev)
        here = lax.broadcasted_iota(jnp.int32, (node_dev, group_rows), 0) + at
        pick = jnp.where(here.astype(f32) == where, 1.0, 0.0).astype(bf16)
        panel_hi[pl.ds(at, node_dev), :] = dot(pick, got_hi).astype(bf16)
        panel_lo[pl.ds(at, node_dev), :] = dot(pick, got_lo).astype(bf16)
        return carry

    lax.fori_loop(0, col_devices, place, 0)

    def chunk(i):
        at = pl.multiple_of(i * node_dev, node_dev)
        a, b = tile_hi[pl.ds(at, node_dev), :], tile_lo[pl.ds(at, node_dev), :]
        return dot(a, panel_hi[...]) + dot(a, panel_lo[...]) + dot(b, panel_hi[...])

    def flipped(t):
        fx, fy = 1 - t // 2, 1 - t % 2
        return (y + fy - 2 * y * fy) * 2 + (x + fx - 2 * x * fx)

    def core_copy(t):
        return remote(sent_part.at[t], core_part.at[t], cs.at[t], cr.at[t], row=at_core)

    def to_pair(t, carry):
        sent_part[t] = chunk(flipped(t) * 2 + 1 - core)
        core_copy(t).start()
        return carry

    lax.fori_loop(0, 4, to_pair, 0)

    def x_copy(t):
        f = 1 - t % 2
        return remote(summed.at[t, pl.ds(0, half)], from_x.at[f], xs.at[f], xr.at[f], row=at_x)

    def y_copy(t):
        f = 1 - t // 2
        return remote(summed.at[t, pl.ds(half, half)], from_y.at[f], ys.at[f], yr.at[f], row=at_y)

    for t in range(4):
        own = chunk(flipped(t) * 2 + core)
        core_copy(t).wait_recv()
        summed[t] = own + core_part[t]
        if t < 2:
            x_copy(t).start()
        if t % 2 == 0:
            y_copy(t).start()
    x_copy(0).wait_recv()
    turned[0] = summed[2, 0:half] + from_x[1]
    late_y = remote(turned.at[0], late.at[0], ls.at[0], lr.at[0], row=at_y)
    late_y.start()
    y_copy(0).wait_recv()
    turned[1] = summed[1, half:] + from_y[1]
    late_x = remote(turned.at[1], late.at[1], ls.at[1], lr.at[1], row=at_x)
    late_x.start()
    x_copy(1).wait_recv()
    y_copy(2).wait_recv()
    late_y.wait_recv()
    late_x.wait_recv()
    hidden = jnp.concatenate(
        [summed[3, 0:half] + from_x[0] + late[0], summed[3, half:] + from_y[0] + late[1]], axis=0
    )

    w = weight[...]
    preact = exact(hidden, w) + bias[...]
    squashed = jax.nn.sigmoid(preact)
    out[...] = preact * squashed
    grad_pre = cotan[...] * squashed * (1.0 + preact * (1.0 - squashed))
    column[row] = lax.dot_general(
        w, grad_pre, (((1,), (1,)), ((), ())), precision=precise, preferred_element_type=f32
    )

    def gather(k, frm, to):
        return remote(column.at[frm], column.at[frm], ags.at[k], agr.at[k], row=to)

    def diag(k, frm, to):
        part = pl.ds(k * half, half)
        return remote(column.at[frm, part], column.at[frm, part], ds.at[k], dr.at[k], row=to)

    def pair(k, frm):
        return remote(column.at[frm], column.at[frm], ks.at[k], kr.at[k], row=at_core)

    other = 1 - 2 * core
    sends = [gather(0, row, at_x), gather(1, row, at_y), pair(0, row)]
    for c in sends:
        c.start()

    local_w = exact(hidden.T, grad_pre)
    local_b = jnp.broadcast_to(jnp.sum(grad_pre, axis=0, keepdims=True), (8, width))
    wper = width // row_devices
    for d in range(row_devices):
        w_sent[d, 0:wper] = local_w[d * wper:(d + 1) * wper]
        w_sent[d, wper:] = local_b
    w_came[row] = w_sent[row]

    def narrowed(i):
        hi, lo = split(column[i])
        at = pl.multiple_of(i * node_dev, node_dev)
        column_hi[:, pl.ds(at, node_dev)] = hi
        column_lo[:, pl.ds(at, node_dev)] = lo

    gather(1, at_y, at_y).wait_recv()
    more = [diag(0, at_y, at_x), pair(1, at_y)]
    for c in more:
        c.start()
    sends += more
    gather(0, at_x, at_x).wait_recv()
    more = [diag(1, at_x, at_y), pair(2, at_x)]
    for c in more:
        c.start()
    sends += more
    for t in range(1, row_devices):
        to = (row + t) % row_devices
        c = remote(w_sent.at[to], w_came.at[row], ws.at[t], wr.at[t], row=to)
        c.start()
        sends.append(c)
    narrowed(row)
    narrowed(at_y)
    narrowed(at_x)
    diag(0, at_diag, at_x).wait_recv()
    diag(1, at_diag, at_y).wait_recv()
    c = pair(3, at_diag)
    c.start()
    sends.append(c)
    narrowed(at_diag)
    for k, frm in enumerate((row, at_y, at_x, at_diag)):
        pair(k, frm + other).wait_recv()
        narrowed(frm + other)

    def back(j):
        at = pl.multiple_of(j * node_dev, node_dev)
        a, b = tile_hi[:, pl.ds(at, node_dev)], tile_lo[:, pl.ds(at, node_dev)]
        return dot(column_hi[...], a) + dot(column_lo[...], a) + dot(column_hi[...], b)

    def x_line(t):
        return remote(sent_x.at[t], came_x.at[t], gs.at[t], gr.at[t], col=(col + t + 1) % col_devices)

    def to_line(t, carry):
        sent_x[t] = back((col + t + 1) % col_devices)

        @pl.when(t < col_devices - 1)
        def _():
            x_line(t).start()

        return carry

    lax.fori_loop(0, col_devices, to_line, 0)

    for t in range(1, row_devices):
        frm = (row + row_devices - t) % row_devices
        remote(w_sent.at[frm], w_came.at[frm], ws.at[t], wr.at[t], row=frm).wait_recv()
    total = w_came[0]
    for s in range(1, row_devices):
        total = total + w_came[s]
    w_line[col] = total
    for t in range(1, col_devices):
        c = remote(w_line.at[col], w_line.at[col], wls.at[t], wlr.at[t], col=(col + t) % col_devices)
        c.start()
        sends.append(c)
    for t in range(1, col_devices):
        frm = (col + col_devices - t) % col_devices
        remote(w_line.at[col], w_line.at[frm], wls.at[t], wlr.at[t], col=frm).wait_recv()
    total = w_line[0]
    for s in range(1, col_devices):
        total = total + w_line[s]
    norm_scale = 1.0 / math.sqrt(node_dev * row_devices * col_devices)
    w_full[row] = total * norm_scale
    for t in range(1, row_devices):
        to = (row + t) % row_devices
        c = remote(w_full.at[row], w_full.at[row], wfs.at[t], wfr.at[t], row=to)
        c.start()
        sends.append(c)
    for t in range(1, row_devices):
        frm = (row + row_devices - t) % row_devices
        remote(w_full.at[row], w_full.at[frm], wfs.at[t], wfr.at[t], row=frm).wait_recv()
    for d in range(row_devices):
        grad_w[d * wper:(d + 1) * wper, :] = w_full[d, 0:wper]
    grad_b[...] = w_full[0, wper:]

    for t in range(col_devices - 1):
        x_line(t).wait_recv()
    total = sent_x[col_devices - 1]
    for t in range(col_devices - 1):
        total = total + came_x[t]
    grad_x[...] = total.T

    for c in first + second + sends:
        c.wait_send()
    for t in range(4):
        core_copy(t).wait_send()
    for t in (0, 1):
        x_copy(t).wait_send()
    for t in (0, 2):
        y_copy(t).wait_send()
    late_y.wait_send()
    late_x.wait_send()
    for t in range(col_devices - 1):
        x_line(t).wait_send()


def in_one_kernel(
    features,
    loader_perm,
    block_values,
    block_row,
    block_column,
    tile_count,
    weight,
    bias_vector,
    cotangent,
):
    node_dev, width = features.shape
    rows, cols = lax.axis_size("row"), lax.axis_size("col")
    _, _, slots, entries = block_values.shape
    side = math.isqrt(entries)
    half, per = node_dev // 2, node_dev // rows
    high, wide = rows * node_dev, cols * node_dev
    wper = width // rows + 8
    f32, bf16 = jnp.float32, jnp.bfloat16
    ids = loader_perm.astype(f32)
    vmem = pl.BlockSpec(memory_space=pltpu.VMEM)
    dma = pltpu.SemaphoreType.DMA
    V = pltpu.VMEM
    square = (node_dev, width)
    out, grad_x, grad_w, grad_b = pl.pallas_call(
        functools.partial(fused, node_dev, rows, cols, side),
        out_shape=(
            jax.ShapeDtypeStruct(square, f32),
            jax.ShapeDtypeStruct(square, f32),
            jax.ShapeDtypeStruct((width, width), f32),
            jax.ShapeDtypeStruct((8, width), f32),
        ),
        in_specs=[vmem] * 6 + [pl.BlockSpec(memory_space=pl.ANY)] + [vmem] * 3,
        out_specs=(vmem,) * 4,
        scratch_shapes=[
            V((rows, per, width), f32), V((rows, 1, 128), f32),
            V((cols, rows, per, width), f32), V((cols, rows, 1, 128), f32),
            V((slots, entries), f32), V((wide // 128, high, 128), f32),
            V((high, wide), bf16), V((high, wide), bf16),
            V((wide, width), bf16), V((wide, width), bf16),
            V((4,) + square, f32), V((4,) + square, f32), V((4,) + square, f32),
            V((2, half, width), f32), V((2, half, width), f32),
            V((2, half, width), f32), V((2, half, width), f32),
            V((rows, width, node_dev), f32),
            V((width, high), bf16), V((width, high), bf16),
            V((cols, width, node_dev), f32), V((cols - 1, width, node_dev), f32),
            V((rows, wper, width), f32), V((rows, wper, width), f32),
            V((cols, wper, width), f32), V((rows, wper, width), f32),
            dma,
            dma((rows,)), dma((rows,)), dma((rows,)), dma((rows,)),
            dma((cols,)), dma((cols,)), dma((cols,)), dma((cols,)),
            dma((4,)), dma((4,)), dma((2,)), dma((2,)), dma((2,)), dma((2,)), dma((2,)), dma((2,)),
            dma((2,)), dma((2,)), dma((2,)), dma((2,)), dma((4,)), dma((4,)),
            dma((cols,)), dma((cols,)), dma((rows,)), dma((rows,)),
            dma((cols,)), dma((cols,)), dma((rows,)), dma((rows,)),
        ],
        compiler_params=pltpu.CompilerParams(
            collective_id=0, has_side_effects=True, vmem_limit_bytes=58 * 2**20
        ),
    )(
        ids.reshape(1, node_dev),
        ids.reshape(node_dev, 1),
        block_row.reshape(1, slots),
        block_column.reshape(1, slots),
        tile_count,
        features,
        block_values.reshape(slots, entries),
        weight,
        bias_vector.reshape(1, width),
        cotangent,
    )
    return (out, grad_x, grad_w, grad_b[0])


def solution(mesh):
    in_specs = (
        P(("row", "col"), None),
        P(("row", "col")),
        P("row", "col", None, None),
        P("row", "col", None),
        P("row", "col", None),
        P("row", "col"),
        P(),
        P(),
        P(("row", "col"), None),
    )
    out_specs = (P(("row", "col"), None), P(("row", "col"), None), P(), P())
    small = mesh.shape["row"] == 8 and mesh.shape["col"] == 4
    return jax.shard_map(
        in_one_kernel if small else general,
        mesh=mesh, in_specs=in_specs, out_specs=out_specs, check_vma=False,
    )
```

```python
import functools
import math

import jax
import jax.numpy as jnp
from jax import lax
from jax.experimental import pallas as pl
from jax.experimental.pallas import tpu as pltpu
from jax.sharding import PartitionSpec as P

precise = lax.Precision.HIGHEST
three = lax.Precision.HIGH


def general(
    features,
    loader_perm,
    block_values,
    block_row,
    block_column,
    tile_count,
    weight,
    bias_vector,
    cotangent,
):
    node_dev, feat_width = features.shape
    row_devices = lax.axis_size("row")
    col_devices = lax.axis_size("col")
    devices = row_devices * col_devices
    row_index = lax.axis_index("row")
    group_rows = col_devices * node_dev
    tile_vals = block_values[0, 0]
    slots, entries = tile_vals.shape
    side = math.isqrt(entries)
    out_blocks = row_devices * node_dev // side
    in_blocks = group_rows // side
    per_group = node_dev // row_devices
    ordering = jnp.argsort(loader_perm // group_rows, stable=True)
    sent_rows = jnp.broadcast_to(
        features[ordering].reshape(row_devices, 1, per_group, feat_width),
        (row_devices, col_devices, per_group, feat_width),
    ).reshape(devices, per_group, feat_width)
    sent_ids = jnp.broadcast_to(
        loader_perm[ordering].astype(jnp.float32).reshape(row_devices, 1, per_group),
        (row_devices, col_devices, per_group),
    ).reshape(devices, per_group)
    got_rows, got_ids = (
        lax.all_to_all(sent_rows, ("row", "col"), split_axis=0, concat_axis=0, tiled=True),
        lax.all_to_all(sent_ids, ("row", "col"), split_axis=0, concat_axis=0, tiled=True),
    )
    spot = block_row[0, 0] * in_blocks + block_column[0, 0]
    alive = jnp.arange(slots, dtype=jnp.int32) < tile_count[0, 0]
    places = jnp.arange(out_blocks * in_blocks, dtype=jnp.int32)
    chosen = ((places[:, None] == spot[None, :]) & alive[None, :]).astype(jnp.float32)
    dense = jnp.dot(chosen, tile_vals, precision=three)
    dense = dense.reshape(out_blocks, in_blocks, side, side).transpose(0, 2, 1, 3)
    dense = dense.reshape(out_blocks * side, in_blocks * side)

    local_pos = got_ids.reshape(group_rows).astype(jnp.int32) - row_index * group_rows
    at = jnp.arange(group_rows, dtype=jnp.int32)
    panel = jnp.dot(
        (at[:, None] == local_pos[None, :]).astype(jnp.float32),
        got_rows.reshape(group_rows, feat_width),
        precision=precise,
    )
    partial_value = jnp.dot(dense, panel, precision=three)
    hidden = lax.psum_scatter(partial_value, "row", scatter_dimension=0, tiled=True)
    preact = jnp.dot(hidden, weight, precision=precise) + bias_vector
    squashed = jax.nn.sigmoid(preact)
    output = preact * squashed
    grad_pre = cotangent * squashed * (1.0 + preact * (1.0 - squashed))
    grad_hidden = jnp.dot(grad_pre, weight.T, precision=precise)
    column = lax.all_gather(grad_hidden, "row", axis=0, tiled=True)
    local_w = jnp.einsum("nf,ng->fg", hidden, grad_pre, precision=precise)
    local_b = jnp.sum(grad_pre, axis=0)
    grad_w, grad_b = lax.psum((local_w, local_b), ("row", "col"))
    partial_x = jnp.einsum("nm,nf->mf", dense, column, precision=three)
    grad_x = lax.psum_scatter(partial_x, "col", scatter_dimension=0, tiled=True)
    norm_scale = 1.0 / math.sqrt(node_dev * devices)
    return (output, grad_x, grad_w * norm_scale, grad_b * norm_scale)


def fused(
    node_dev, row_devices, col_devices, side,
    ids_row, ids_col, blk_row, blk_col, live, feats, vals_hbm, weight, bias, cotan,
    out, grad_x, grad_w, grad_b,
    sorted_rows, sorted_ids, got, got_ids, vals, tall, tile_hi, tile_lo, panel_hi, panel_lo,
    sent_part, core_part, summed, from_x, from_y, turned, late,
    column, column_hi, column_lo, sent_x, came_x, w_sent, w_came, w_line, w_full,
    vals_sem, fs, fr, fis, fir, zs, zr, zis, zir, cs, cr, xs, xr, ys, yr, ls, lr,
    ags, agr, ds, dr, ks, kr, gs, gr, ws, wr, wls, wlr, wfs, wfr,
):
    width = weight.shape[0]
    row, col = lax.axis_index("row"), lax.axis_index("col")
    core, chip = row % 2, row // 2
    x, y = chip % 2, chip // 2
    at_core = row + 1 - 2 * core
    at_x = row + 2 - 4 * x
    at_y = row + 4 - 8 * y
    at_diag = at_x + 4 - 8 * y
    half = node_dev // 2
    group_rows = col_devices * node_dev
    per = node_dev // row_devices
    slots = vals.shape[0]
    f32, bf16 = jnp.float32, jnp.bfloat16

    def remote(src, dst, ssem, rsem, **where):
        return pltpu.make_async_remote_copy(
            src_ref=src, dst_ref=dst, send_sem=ssem, recv_sem=rsem,
            device_id=where, device_id_type=pl.DeviceIdType.MESH,
        )

    def dot(a, b):
        return jnp.dot(a, b, preferred_element_type=f32)

    def exact(a, b):
        return jnp.dot(a, b, precision=precise, preferred_element_type=f32)

    def split(a):
        hi = a.astype(bf16)
        return hi, (a - hi.astype(f32)).astype(bf16)

    fetch = pltpu.make_async_copy(vals_hbm, vals, vals_sem)
    fetch.start()

    barrier = pltpu.get_barrier_semaphore()
    for t in range(1, row_devices):
        pl.semaphore_signal(
            barrier, inc=1, device_id={"row": (row + t) % row_devices},
            device_id_type=pl.DeviceIdType.MESH,
        )
    for t in range(1, col_devices):
        pl.semaphore_signal(
            barrier, inc=1, device_id={"col": (col + t) % col_devices},
            device_id_type=pl.DeviceIdType.MESH,
        )

    idr, idc = ids_row[...], ids_col[...]
    scale = 1.0 / group_rows
    grp_r, grp_c = jnp.floor(idr * scale), jnp.floor(idc * scale)
    sub = lax.broadcasted_iota(jnp.int32, (node_dev, node_dev), 0)
    lane = lax.broadcasted_iota(jnp.int32, (node_dev, node_dev), 1)
    same = grp_c == grp_r
    rank_r = jnp.sum(jnp.where(same & (sub < lane), 1.0, 0.0), axis=0, keepdims=True)
    rank_c = jnp.sum(jnp.where(same & (lane < sub), 1.0, 0.0), axis=1, keepdims=True)
    slot_r = grp_r * per + rank_r
    order = jnp.where(sub.astype(f32) == slot_r, 1.0, 0.0)
    moved = exact(order, feats[...])
    packed = 128 // per
    lane128 = lax.broadcasted_iota(jnp.int32, (node_dev, 128), 1)
    shift = ((row % packed) * per).astype(f32)
    placed = jnp.where(lane128.astype(f32) == rank_c + shift, 1.0, 0.0)
    dest = lax.broadcasted_iota(jnp.int32, (row_devices, node_dev), 0).astype(f32)
    id_rows = exact(jnp.where(dest == grp_r, idr, 0.0), placed)
    for d in range(row_devices):
        sorted_rows[d] = moved[d * per:(d + 1) * per]
        sorted_ids[d] = id_rows[d:d + 1]
    got[col, row] = sorted_rows[row]
    got_ids[col, row] = sorted_ids[row]

    pl.semaphore_wait(barrier, row_devices - 1 + col_devices - 1)
    first = []
    for t in range(1, row_devices):
        to = (row + t) % row_devices
        a = remote(sorted_rows.at[to], got.at[col, row], fs.at[t], fr.at[t], row=to)
        b = remote(sorted_ids.at[to], got_ids.at[col, row], fis.at[t], fir.at[t], row=to)
        a.start()
        b.start()
        first += [a, b]

    fetch.wait()

    count = live[...]
    slot_at = lax.broadcasted_iota(jnp.int32, (1, slots), 1)
    out_blocks = row_devices * node_dev // side
    in_blocks = group_rows // side
    key = jnp.where(slot_at < count, blk_col[...] * out_blocks + blk_row[...], -1)
    spot = lax.broadcasted_iota(jnp.int32, (out_blocks * in_blocks, slots), 0)
    chosen = jnp.where(spot == key, 1.0, 0.0).astype(bf16)
    left = lax.broadcasted_iota(jnp.int32, (out_blocks, 128), 1) < side

    def densify(step, carry):
        part = vals[:, pl.ds(pl.multiple_of(step * 256, 256), 256)]
        hi, lo = split(part)
        dense = dot(chosen, hi) + dot(chosen, lo)
        for pair in range(in_blocks // 2):
            top = dense[(2 * pair) * out_blocks:(2 * pair + 1) * out_blocks]
            low = dense[(2 * pair + 1) * out_blocks:(2 * pair + 2) * out_blocks]
            for h in range(2):
                p0, p1 = top[:, h * 128:(h + 1) * 128], low[:, h * 128:(h + 1) * 128]
                even = jnp.where(left, p0, pltpu.roll(p1, side, 1))
                odd = jnp.where(left, pltpu.roll(p0, side, 1), p1)
                at = step * 4 + h * 2
                tall[pair, pl.ds(at, out_blocks, stride=side), :] = even
                tall[pair, pl.ds(at + 1, out_blocks, stride=side), :] = odd
        return carry

    steps = vals.shape[1] // 256
    lax.fori_loop(0, steps // 8, densify, 0)

    for t in range(1, row_devices):
        frm = (row + row_devices - t) % row_devices
        remote(sorted_rows.at[frm], got.at[col, frm], fs.at[t], fr.at[t], row=frm).wait_recv()
        remote(sorted_ids.at[frm], got_ids.at[col, frm], fis.at[t], fir.at[t], row=frm).wait_recv()
    second = []
    for t in range(1, col_devices):
        to = (col + t) % col_devices
        a = remote(got.at[col], got.at[col], zs.at[t], zr.at[t], col=to)
        b = remote(got_ids.at[col], got_ids.at[col], zis.at[t], zir.at[t], col=to)
        a.start()
        b.start()
        second += [a, b]

    lax.fori_loop(steps // 8, steps, densify, 0)

    def narrow(i, carry):
        at = pl.multiple_of(i * node_dev, node_dev)
        for pair in range(in_blocks // 2):
            hi, lo = split(tall[pair, pl.ds(at, node_dev), :])
            tile_hi[pl.ds(at, node_dev), pair * 128:(pair + 1) * 128] = hi
            tile_lo[pl.ds(at, node_dev), pair * 128:(pair + 1) * 128] = lo
        return carry

    lax.fori_loop(0, row_devices, narrow, 0)

    for t in range(1, col_devices):
        frm = (col + col_devices - t) % col_devices
        remote(got.at[col], got.at[frm], zs.at[t], zr.at[t], col=frm).wait_recv()
        remote(got_ids.at[col], got_ids.at[frm], zis.at[t], zir.at[t], col=frm).wait_recv()

    pieces = []
    for j in range(col_devices):
        for s in range(0, row_devices, packed):
            pieces.append(sum(got_ids[j, s + k] for k in range(packed)))
    where = jnp.concatenate(pieces, axis=1) - (row * group_rows).astype(f32)
    got_hi, got_lo = split(got[...].reshape(group_rows, width))

    def place(i, carry):
        at = pl.multiple_of(i * node_dev, node_dev)
        here = lax.broadcasted_iota(jnp.int32, (node_dev, group_rows), 0) + at
        pick = jnp.where(here.astype(f32) == where, 1.0, 0.0).astype(bf16)
        panel_hi[pl.ds(at, node_dev), :] = dot(pick, got_hi).astype(bf16)
        panel_lo[pl.ds(at, node_dev), :] = dot(pick, got_lo).astype(bf16)
        return carry

    lax.fori_loop(0, col_devices, place, 0)

    def chunk(i):
        at = pl.multiple_of(i * node_dev, node_dev)
        a, b = tile_hi[pl.ds(at, node_dev), :], tile_lo[pl.ds(at, node_dev), :]
        return dot(a, panel_hi[...]) + dot(a, panel_lo[...]) + dot(b, panel_hi[...])

    def flipped(t):
        fx, fy = 1 - t // 2, 1 - t % 2
        return (y + fy - 2 * y * fy) * 2 + (x + fx - 2 * x * fx)

    def core_copy(t):
        return remote(sent_part.at[t], core_part.at[t], cs.at[t], cr.at[t], row=at_core)

    def to_pair(t, carry):
        sent_part[t] = chunk(flipped(t) * 2 + 1 - core)
        core_copy(t).start()
        return carry

    lax.fori_loop(0, 4, to_pair, 0)

    def x_copy(t):
        f = 1 - t % 2
        return remote(summed.at[t, pl.ds(0, half)], from_x.at[f], xs.at[f], xr.at[f], row=at_x)

    def y_copy(t):
        f = 1 - t // 2
        return remote(summed.at[t, pl.ds(half, half)], from_y.at[f], ys.at[f], yr.at[f], row=at_y)

    for t in range(4):
        own = chunk(flipped(t) * 2 + core)
        core_copy(t).wait_recv()
        summed[t] = own + core_part[t]
        if t < 2:
            x_copy(t).start()
        if t % 2 == 0:
            y_copy(t).start()
    x_copy(0).wait_recv()
    turned[0] = summed[2, 0:half] + from_x[1]
    late_y = remote(turned.at[0], late.at[0], ls.at[0], lr.at[0], row=at_y)
    late_y.start()
    y_copy(0).wait_recv()
    turned[1] = summed[1, half:] + from_y[1]
    late_x = remote(turned.at[1], late.at[1], ls.at[1], lr.at[1], row=at_x)
    late_x.start()
    x_copy(1).wait_recv()
    y_copy(2).wait_recv()
    late_y.wait_recv()
    late_x.wait_recv()
    hidden = jnp.concatenate(
        [summed[3, 0:half] + from_x[0] + late[0], summed[3, half:] + from_y[0] + late[1]], axis=0
    )

    w = weight[...]
    preact = exact(hidden, w) + bias[...]
    squashed = jax.nn.sigmoid(preact)
    out[...] = preact * squashed
    grad_pre = cotan[...] * squashed * (1.0 + preact * (1.0 - squashed))
    column[row] = lax.dot_general(
        w, grad_pre, (((1,), (1,)), ((), ())), precision=precise, preferred_element_type=f32
    )

    def gather(k, frm, to):
        return remote(column.at[frm], column.at[frm], ags.at[k], agr.at[k], row=to)

    def diag(k, frm, to):
        part = pl.ds(k * half, half)
        return remote(column.at[frm, part], column.at[frm, part], ds.at[k], dr.at[k], row=to)

    def pair(k, frm):
        return remote(column.at[frm], column.at[frm], ks.at[k], kr.at[k], row=at_core)

    other = 1 - 2 * core
    sends = [gather(0, row, at_x), gather(1, row, at_y), pair(0, row)]
    for c in sends:
        c.start()

    local_w = exact(hidden.T, grad_pre)
    local_b = jnp.broadcast_to(jnp.sum(grad_pre, axis=0, keepdims=True), (8, width))
    wper = width // row_devices
    for d in range(row_devices):
        w_sent[d, 0:wper] = local_w[d * wper:(d + 1) * wper]
        w_sent[d, wper:] = local_b
    w_came[row] = w_sent[row]

    def narrowed(i):
        hi, lo = split(column[i])
        at = pl.multiple_of(i * node_dev, node_dev)
        column_hi[:, pl.ds(at, node_dev)] = hi
        column_lo[:, pl.ds(at, node_dev)] = lo

    gather(1, at_y, at_y).wait_recv()
    more = [diag(0, at_y, at_x), pair(1, at_y)]
    for c in more:
        c.start()
    sends += more
    gather(0, at_x, at_x).wait_recv()
    more = [diag(1, at_x, at_y), pair(2, at_x)]
    for c in more:
        c.start()
    sends += more
    for t in range(1, row_devices):
        to = (row + t) % row_devices
        c = remote(w_sent.at[to], w_came.at[row], ws.at[t], wr.at[t], row=to)
        c.start()
        sends.append(c)
    narrowed(row)
    narrowed(at_y)
    narrowed(at_x)
    diag(0, at_diag, at_x).wait_recv()
    diag(1, at_diag, at_y).wait_recv()
    c = pair(3, at_diag)
    c.start()
    sends.append(c)
    narrowed(at_diag)
    for k, frm in enumerate((row, at_y, at_x, at_diag)):
        pair(k, frm + other).wait_recv()
        narrowed(frm + other)

    def back(j):
        at = pl.multiple_of(j * node_dev, node_dev)
        a, b = tile_hi[:, pl.ds(at, node_dev)], tile_lo[:, pl.ds(at, node_dev)]
        return dot(column_hi[...], a) + dot(column_lo[...], a) + dot(column_hi[...], b)

    def x_line(t):
        return remote(sent_x.at[t], came_x.at[t], gs.at[t], gr.at[t], col=(col + t + 1) % col_devices)

    def to_line(t, carry):
        sent_x[t] = back((col + t + 1) % col_devices)

        @pl.when(t < col_devices - 1)
        def _():
            x_line(t).start()

        return carry

    for t in range(1, row_devices):
        frm = (row + row_devices - t) % row_devices
        remote(w_sent.at[frm], w_came.at[frm], ws.at[t], wr.at[t], row=frm).wait_recv()
    total = w_came[0]
    for s in range(1, row_devices):
        total = total + w_came[s]
    w_line[col] = total
    for t in range(1, col_devices):
        c = remote(w_line.at[col], w_line.at[col], wls.at[t], wlr.at[t], col=(col + t) % col_devices)
        c.start()
        sends.append(c)
    lax.fori_loop(0, col_devices, to_line, 0)

    for t in range(1, col_devices):
        frm = (col + col_devices - t) % col_devices
        remote(w_line.at[col], w_line.at[frm], wls.at[t], wlr.at[t], col=frm).wait_recv()
    total = w_line[0]
    for s in range(1, col_devices):
        total = total + w_line[s]
    norm_scale = 1.0 / math.sqrt(node_dev * row_devices * col_devices)
    w_full[row] = total * norm_scale
    for t in range(1, row_devices):
        to = (row + t) % row_devices
        c = remote(w_full.at[row], w_full.at[row], wfs.at[t], wfr.at[t], row=to)
        c.start()
        sends.append(c)
    for t in range(1, row_devices):
        frm = (row + row_devices - t) % row_devices
        remote(w_full.at[row], w_full.at[frm], wfs.at[t], wfr.at[t], row=frm).wait_recv()
    for d in range(row_devices):
        grad_w[d * wper:(d + 1) * wper, :] = w_full[d, 0:wper]
    grad_b[...] = w_full[0, wper:wper + 1]

    for t in range(col_devices - 1):
        x_line(t).wait_recv()
    total = sent_x[col_devices - 1]
    for t in range(col_devices - 1):
        total = total + came_x[t]
    grad_x[...] = total.T

    for c in first + second + sends:
        c.wait_send()
    for t in range(4):
        core_copy(t).wait_send()
    for t in (0, 1):
        x_copy(t).wait_send()
    for t in (0, 2):
        y_copy(t).wait_send()
    late_y.wait_send()
    late_x.wait_send()
    for t in range(col_devices - 1):
        x_line(t).wait_send()


def in_one_kernel(
    features,
    loader_perm,
    block_values,
    block_row,
    block_column,
    tile_count,
    weight,
    bias_vector,
    cotangent,
):
    node_dev, width = features.shape
    rows, cols = lax.axis_size("row"), lax.axis_size("col")
    _, _, slots, entries = block_values.shape
    side = math.isqrt(entries)
    half, per = node_dev // 2, node_dev // rows
    high, wide = rows * node_dev, cols * node_dev
    wper = width // rows + 8
    f32, bf16 = jnp.float32, jnp.bfloat16
    ids = loader_perm.astype(f32)
    vmem = pl.BlockSpec(memory_space=pltpu.VMEM)
    dma = pltpu.SemaphoreType.DMA
    V = pltpu.VMEM
    square = (node_dev, width)
    out, grad_x, grad_w, grad_b = pl.pallas_call(
        functools.partial(fused, node_dev, rows, cols, side),
        out_shape=(
            jax.ShapeDtypeStruct(square, f32),
            jax.ShapeDtypeStruct(square, f32),
            jax.ShapeDtypeStruct((width, width), f32),
            jax.ShapeDtypeStruct((1, width), f32),
        ),
        in_specs=[vmem] * 6 + [pl.BlockSpec(memory_space=pl.ANY)] + [vmem] * 3,
        out_specs=(vmem,) * 4,
        scratch_shapes=[
            V((rows, per, width), f32), V((rows, 1, 128), f32),
            V((cols, rows, per, width), f32), V((cols, rows, 1, 128), f32),
            V((slots, entries), f32), V((wide // 128, high, 128), f32),
            V((high, wide), bf16), V((high, wide), bf16),
            V((wide, width), bf16), V((wide, width), bf16),
            V((4,) + square, f32), V((4,) + square, f32), V((4,) + square, f32),
            V((2, half, width), f32), V((2, half, width), f32),
            V((2, half, width), f32), V((2, half, width), f32),
            V((rows, width, node_dev), f32),
            V((width, high), bf16), V((width, high), bf16),
            V((cols, width, node_dev), f32), V((cols - 1, width, node_dev), f32),
            V((rows, wper, width), f32), V((rows, wper, width), f32),
            V((cols, wper, width), f32), V((rows, wper, width), f32),
            dma,
            dma((rows,)), dma((rows,)), dma((rows,)), dma((rows,)),
            dma((cols,)), dma((cols,)), dma((cols,)), dma((cols,)),
            dma((4,)), dma((4,)), dma((2,)), dma((2,)), dma((2,)), dma((2,)), dma((2,)), dma((2,)),
            dma((2,)), dma((2,)), dma((2,)), dma((2,)), dma((4,)), dma((4,)),
            dma((cols,)), dma((cols,)), dma((rows,)), dma((rows,)),
            dma((cols,)), dma((cols,)), dma((rows,)), dma((rows,)),
        ],
        compiler_params=pltpu.CompilerParams(
            collective_id=0, has_side_effects=True, vmem_limit_bytes=58 * 2**20
        ),
    )(
        ids.reshape(1, node_dev),
        ids.reshape(node_dev, 1),
        block_row.reshape(1, slots),
        block_column.reshape(1, slots),
        tile_count,
        features,
        block_values.reshape(slots, entries),
        weight,
        bias_vector.reshape(1, width),
        cotangent,
    )
    return (out, grad_x, grad_w, grad_b.reshape(width))


def solution(mesh):
    in_specs = (
        P(("row", "col"), None),
        P(("row", "col")),
        P("row", "col", None, None),
        P("row", "col", None),
        P("row", "col", None),
        P("row", "col"),
        P(),
        P(),
        P(("row", "col"), None),
    )
    out_specs = (P(("row", "col"), None), P(("row", "col"), None), P(), P())
    small = mesh.shape["row"] == 8 and mesh.shape["col"] == 4
    return jax.shard_map(
        in_one_kernel if small else general,
        mesh=mesh, in_specs=in_specs, out_specs=out_specs, check_vma=False,
    )
```
